32 devices in a mesh: row: 4 (over y, core), col: 8 (over z, x).
Axes of the slice: x: 2, y: 2, z: 4, core: 2. Of those that a mesh axis runs over, the one named last changes fastest.
Arguments:
- positions: float32 [4, 4096, 4096], P(None, 'row', 'col'), may hold values from -2 to 2, as said below
Outputs:
- rotated: float32 [4, 4096, 4096], P(None, 'row', 'col')
The draws below stay inside these ranges and needn't reach their ends.
Inputs may be any that keep to these rules, and one draw needn't show every extreme that they name: `positions`: each of the 4 matrices is symmetric.
All inputs are finite; a program needn't handle non-finite values.
Results may differ from the reference program's by a relative error of at most 0.00026.
Values sent between devices are 32-bit elements; how exact they have to be, the bound alone decides.
No kernel may reach another device: no remote copies, remote signals or barrier semaphores. Data moves between devices by JAX's collectives and lax.ppermute only.
A program may use at most 256 MiB of HBM per device.

```python
import jax
import jax.numpy as jnp
import numpy as np
from jax import lax

N = 4096
KMAT = 4
TERMS = 4
BLOCK = 512
N_COL = 8


def draw_positions(key, part):
    keys = jax.random.split(key, 3)
    spread = N ** (-0.5)
    raw = jax.random.truncated_normal(keys[0], -4.0, 4.0, (KMAT, N, N), jnp.float32)
    centres = jax.random.uniform(keys[2], (KMAT, N), jnp.float32, -1.5, 1.5)
    upper_part = jnp.triu(raw * spread, 1)
    identity = jnp.eye(N, dtype=jnp.float32)
    return upper_part + jnp.swapaxes(upper_part, 1, 2) + centres[:, :, None] * identity[None, :, :]


def setup_inputs(seed: int = 0) -> dict:
    arg_keys = jax.random.split(jax.random.key(seed), 2)
    return {
        "positions": draw_positions(jax.random.fold_in(arg_keys[1], 71), 0),
    }


STEP_SIZE = 0.4
HIGHEST = lax.Precision.HIGHEST


def pair_indices(stride):
    leaders = [first_block for first_block in range(N_COL) if first_block % (2 * stride) < stride]
    rows_of = []
    for first_block in leaders:
        lower_rows = np.arange(first_block * BLOCK, (first_block + 1) * BLOCK)
        upper_rows = np.arange((first_block + stride) * BLOCK, (first_block + stride + 1) * BLOCK)
        rows_of.append(np.concatenate([lower_rows, upper_rows]))
    return np.stack(rows_of).astype(np.int32)


def taylor_series(generator):
    pair_width = generator.shape[-1]
    identity = jnp.broadcast_to(jnp.eye(pair_width, dtype=generator.dtype), generator.shape)
    current = identity
    summed = identity
    for power in range(1, TERMS + 1):
        current = jnp.einsum('pij,pjk->pik', generator, current, precision=HIGHEST) / power
        summed = summed + current
    return summed


def jacobi_round(positions, stride):
    groups = pair_indices(stride)
    pair_count = groups.shape[0]
    pair_width = groups.shape[1]
    order_index = groups.reshape(-1)
    inverse_index = np.argsort(order_index).astype(np.int32)
    diagonal_blocks = positions[:, groups[:, :, None], groups[:, None, :]]
    centres = jnp.diagonal(diagonal_blocks, axis1=2, axis2=3)
    generator = STEP_SIZE * jnp.sum(diagonal_blocks * (centres[:, :, None, :] - centres[:, :, :, None]), axis=0)
    rotation = taylor_series(generator)
    results = []
    for matrix_id in range(KMAT):
        permuted = positions[matrix_id][order_index][:, order_index].reshape(pair_count, pair_width, pair_count, pair_width)
        left_side = jnp.einsum('pia,piqb->paqb', rotation, permuted, precision=HIGHEST)
        both_sides = jnp.einsum('paqj,qjb->paqb', left_side, rotation, precision=HIGHEST)
        results.append(both_sides.reshape(N, N)[inverse_index][:, inverse_index])
    return jnp.stack(results)


def reference(positions):
    round_positions = jacobi_round(positions, 1)
    return jacobi_round(round_positions, N_COL // 2)
```

```python
import functools

import jax
import jax.numpy as jnp
from jax import lax
from jax.experimental import pallas as pl
from jax.experimental.pallas import tpu as pltpu
from jax.sharding import PartitionSpec as P

STEP_SIZE = 0.4
EARLY = 2


def after(value, *earlier):
    return lax.optimization_barrier((value, *earlier))[0]


class Grid:
    def __init__(self, rows, cols):
        self.rows, self.cols = rows, cols
        self.groups = rows // 2
        row_id, col_id = lax.axis_index("row"), lax.axis_index("col")
        self.row_high, self.row_group = row_id // self.groups, row_id % self.groups
        self.col_high = col_id // (cols // 2)
        self.col_group = col_id % (cols // 2) // 2
        self.parity = col_id % 2

    def split(self, row, col):
        half = self.cols // 2
        return row // self.groups, row % self.groups, col // half, col % half // 2, col % 2

    def send(self, value, row_flip, col_flip, chosen=None):
        pairs = []
        for row in range(self.rows):
            for col in range(self.cols):
                if chosen is None or chosen(*self.split(row, col)):
                    target = (row ^ row_flip) * self.cols + (col ^ col_flip)
                    pairs.append((row * self.cols + col, target))
        return lax.ppermute(value, ("row", "col"), pairs)

    def swap_parity(self, value, chosen=None):
        return self.send(value, 0, 1, chosen)

    def swap_col_high(self, value, chosen=None):
        return self.send(value, 0, self.cols // 2, chosen)

    def swap_row_high(self, value, chosen=None):
        return self.send(value, self.rows // 2, 0, chosen)

    def spread_col_group(self, value):
        bit = 1
        while bit < self.groups:
            def holds(rh, rg, ch, cg, e, bit=bit):
                return (rg ^ cg) < bit

            arrived = self.send(value, 0, 2 * bit, holds)
            value = jnp.where((self.row_group ^ self.col_group) & bit != 0, arrived, value)
            bit *= 2
        return value

    def spread_row_group(self, value):
        bit = 1
        while bit < self.groups:
            def holds(rh, rg, ch, cg, e, bit=bit):
                return (rg ^ cg) < bit

            arrived = self.send(value, bit, 0, holds)
            value = jnp.where((self.row_group ^ self.col_group) & bit != 0, arrived, value)
            bit *= 2
        return value


def on_group(rh, rg, ch, cg, e):
    return rg == cg


def off_group(rh, rg, ch, cg, e):
    return rg != cg


def on_pair(rh, rg, ch, cg, e):
    return rg == cg and rh == ch


def triangle_masks(width):
    row = lax.broadcasted_iota(jnp.int32, (width, width), 0)
    col = lax.broadcasted_iota(jnp.int32, (width, width), 1)
    return row, col


def diagonal(blocks):
    row, col = triangle_masks(blocks.shape[-1])
    return jnp.sum(jnp.where((row == col)[None], blocks, 0.0), axis=1)


def halves(value):
    high = value.astype(jnp.bfloat16)
    return high, (value - high.astype(jnp.float32)).astype(jnp.bfloat16)


def three_pass(left_high, left_low, right_high, right_low):
    def dot(a, b):
        return jnp.dot(a, b, preferred_element_type=jnp.float32)

    small = dot(left_high, right_low) + dot(left_low, right_high)
    return dot(left_high, right_high) + small


def rotation_kernel(
    flags_ref, first_ref, second_ref, columns_ref, high_ref, low_ref,
    gen, square_ref, gen_high, gen_low, in_high, in_low,
):
    width = first_ref.shape[0]
    size = 2 * width
    step = min(width, 256)
    first, second = first_ref[...], second_ref[...]
    first_t, second_t = first.T, second.T
    row, col = triangle_masks(width)
    gen[:width, :width] = jnp.where(row < col, first, jnp.where(row > col, -first_t, 0.0))
    gen[width:, width:] = jnp.where(row < col, second, jnp.where(row > col, -second_t, 0.0))
    gen[width:, :width] = jnp.where(row >= col, first, -second_t)
    gen[:width, width:] = jnp.where(row <= col, -first_t, second)
    gen_high[...], gen_low[...] = halves(gen[...])

    def on_eye(index):
        row = lax.broadcasted_iota(jnp.int32, (step, size), 0) + index * step
        return row == lax.broadcasted_iota(jnp.int32, (step, size), 1)

    def square(index, carry):
        rows = pl.ds(pl.multiple_of(index * step, step), step)
        product = three_pass(gen_high[rows, :], gen_low[rows, :], gen_high[...], gen_low[...])
        square_ref[rows, :] = product
        value = gen[rows, :] * (1 / 6) + product * (1 / 24)
        in_high[rows, :], in_low[rows, :] = halves(value + jnp.where(on_eye(index), 0.5, 0.0))
        return carry

    lax.fori_loop(0, size // step, square, 0)
    swap_rows, swap_cols, chosen = flags_ref[0], flags_ref[1], flags_ref[2]

    def outer(index, carry):
        rows = pl.ds(pl.multiple_of(index * step, step), step)
        high, low = halves(square_ref[rows, :])
        product = three_pass(high, low, in_high[...], in_low[...])
        value = product + gen[rows, :] + jnp.where(on_eye(index), 1.0, 0.0)
        columns_ref[rows, :] = jnp.where(chosen == 0, value[:, :width], value[:, width:])
        turned = value.T
        per_half = width // step
        place = (index // per_half + swap_cols) % 2 * per_half + index % per_half
        cols = pl.ds(pl.multiple_of(place * step, step), step)
        for part in range(2):
            start = pl.multiple_of((part + swap_rows) % 2 * width, width)
            high, low = halves(turned[part * width : (part + 1) * width])
            high_ref[pl.ds(start, width), cols] = high
            low_ref[pl.ds(start, width), cols] = low
        return carry

    lax.fori_loop(0, size // step, outer, 0)


NO_COST = pl.CostEstimate(flops=0, bytes_accessed=0, transcendentals=0)


def rotation_of(first, second, swap_rows, swap_cols, chosen):
    width = first.shape[0]
    size = 2 * width
    whole = pl.BlockSpec(memory_space=pltpu.VMEM)
    flags = jnp.stack([jnp.asarray(flag, jnp.int32) for flag in (swap_rows, swap_cols, chosen)])
    return pl.pallas_call(
        rotation_kernel,
        out_shape=(
            jax.ShapeDtypeStruct((size, width), jnp.float32),
            jax.ShapeDtypeStruct((size, size), jnp.bfloat16),
            jax.ShapeDtypeStruct((size, size), jnp.bfloat16),
        ),
        in_specs=[pl.BlockSpec(memory_space=pltpu.SMEM), whole, whole],
        out_specs=(whole, whole, whole),
        scratch_shapes=[pltpu.VMEM((size, size), jnp.float32)] * 2
        + [pltpu.VMEM((size, size), jnp.bfloat16)] * 4,
        compiler_params=pltpu.CompilerParams(vmem_limit_bytes=48 * 2**20),
        cost_estimate=NO_COST,
    )(flags, first, second)


def rotate_kernel(spans, per_half, *refs):
    step = pl.program_id(0)
    at = sum(count for side in spans for _, _, count in side)
    weights, turn_high, turn_low = refs[at : at + 2], refs[at + 2], refs[at + 3]
    outs = refs[at + 4 : -6]
    weight_high, weight_low = refs[-6:-4], refs[-4:-2]
    mid_high, mid_low = refs[-2:]
    block = turn_high.shape[0]
    first_part = 2 * per_half

    @pl.when(step == 0)
    def _():
        for side in range(2):
            weight_high[side][...], weight_low[side][...] = halves(weights[side][...])

    for now in range(first_part):

        @pl.when(step == now)
        def _(now=now):
            total, at = None, 0
            for side in range(2):
                for first, steps, count in spans[side]:
                    if first <= now < first + steps:
                        value = refs[at][...]
                        for ref in refs[at + 1 : at + count]:
                            value = value + ref[...]
                        high, low = halves(value)
                        part = three_pass(high, low, weight_high[side][...], weight_low[side][...])
                        total = part if total is None else total + part
                    at += count
            rows = pl.ds(now * block, block)
            mid_high[rows, :], mid_low[rows, :] = halves(total)

    @pl.when(step >= first_part)
    def _():
        product = three_pass(turn_high[...], turn_low[...], mid_high[...], mid_low[...])
        for half, out in enumerate(outs):

            @pl.when((step - first_part) // per_half == half)
            def _(out=out):
                out[...] = product


def block_rows(width):
    return min(width, 256)


def rotate(near, far, near_weights, far_weights, turn):
    width = near_weights.shape[0]
    size = 2 * width
    block = block_rows(width)
    per_half = width // block
    first_part = 2 * per_half
    turn_high, turn_low = turn
    out_halves = turn_high.shape[0] // width
    arrays, specs, spans = [], [], []
    for side in (near, far):
        span, first = [], 0
        for piece in side:
            steps = piece[0].shape[0] // block
            span.append((first, steps, len(piece)))

            def place(step, first=first, steps=steps):
                return jnp.clip(step - first, 0, steps - 1), 0

            for array in piece:
                arrays.append(array)
                specs.append(pl.BlockSpec((block, width), place))
            first += steps
        spans.append(tuple(span))
    fixed = pl.BlockSpec((width, width), lambda step: (0, 0))
    turning = pl.BlockSpec(
        (block, size),
        lambda step: (jnp.clip(step - first_part, 0, out_halves * per_half - 1), 0),
    )
    outs = [
        pl.BlockSpec(
            (block, width),
            lambda step, half=half: (
                jnp.clip(step - first_part - half * per_half, 0, per_half - 1),
                0,
            ),
        )
        for half in range(out_halves)
    ]
    return pl.pallas_call(
        functools.partial(rotate_kernel, tuple(spans), per_half),
        grid=(first_part + out_halves * per_half,),
        out_shape=[jax.ShapeDtypeStruct((width, width), jnp.float32)] * out_halves,
        in_specs=[*specs, fixed, fixed, turning, turning],
        out_specs=outs,
        scratch_shapes=[pltpu.VMEM((width, width), jnp.bfloat16)] * 4
        + [pltpu.VMEM((size, width), jnp.bfloat16)] * 2,
        compiler_params=pltpu.CompilerParams(vmem_limit_bytes=40 * 2**20),
        cost_estimate=NO_COST,
    )(*arrays, near_weights, far_weights, turn_high, turn_low)


def rows_of(value, which, width):
    return lax.dynamic_slice_in_dim(value, which * width, width, value.ndim - 2)


def first_generator(grid, tiles, own_centres, other_centres):
    width = tiles.shape[2]
    is_first = grid.parity == 0
    centres = jnp.where(
        is_first,
        jnp.concatenate((own_centres, other_centres), axis=1),
        jnp.concatenate((other_centres, own_centres), axis=1),
    )
    generator = STEP_SIZE * jnp.sum(
        tiles * (own_centres[:, None, :] - centres[:, :, None]), axis=0
    )
    row, col = triangle_masks(width)
    top, bottom = generator[:width], generator[width:]
    return jnp.where(
        is_first, jnp.where(row < col, top, bottom), jnp.where(row < col, bottom, top)
    )


def second_generator(grid, blocks, own_centres, row_centres, col_centres):
    same = grid.row_high == grid.col_high
    row_centres = jnp.where(same, own_centres, row_centres)
    col_centres = jnp.where(same, own_centres, col_centres)
    return STEP_SIZE * jnp.sum(
        blocks * (col_centres[:, None, :] - row_centres[:, :, None]), axis=0
    )


def cut(array, block):
    return [array[row : row + block] for row in range(0, array.shape[0], block)]


def take(queue, count):
    taken = queue[:count]
    del queue[:count]
    return taken


def local(positions):
    grid = Grid(lax.axis_size("row"), lax.axis_size("col"))
    count, height, width = positions.shape
    block = block_rows(width)
    pieces_of = height // block
    early, late = list(range(EARLY)), list(range(EARLY, count))
    is_first = grid.parity == 0
    is_low = grid.row_high == 0
    is_left = grid.col_high == 0
    same = grid.row_high == grid.col_high
    groups = grid.groups > 1
    gate = lax.optimization_barrier

    raw_queue = [(k, piece) for k in early for piece in range(pieces_of)]
    far = {k: [] for k in early}

    def send_raw(tiles, number):
        for k, piece in take(raw_queue, number):
            rows = tiles[k, piece * block : (piece + 1) * block]
            far[k].append(grid.swap_col_high(rows))

    def weights_of(columns, which):
        return rows_of(columns, which, width), rows_of(columns, 1 - which, width)

    tiles = positions
    own_centres = diagonal(rows_of(tiles, grid.parity, width))
    other_centres = grid.swap_parity(own_centres, on_pair)
    send_raw(tiles, 1)
    packed = first_generator(grid, tiles, own_centres, other_centres)
    tiles, packed, far = gate((tiles, packed, far))

    urgent = [grid.swap_parity(tiles[0], on_group)]
    packed = jnp.where(same, packed, grid.swap_col_high(packed, on_pair))
    tiles, packed, urgent = gate((tiles, packed, urgent))

    packed = grid.spread_col_group(packed)
    urgent.append(grid.swap_parity(tiles[1], on_group))
    send_raw(tiles, 1)
    tiles, packed, urgent, far = gate((tiles, packed, urgent, far))

    other = grid.swap_parity(packed)
    send_raw(tiles, 1)
    tiles, packed, other, far = gate((tiles, packed, other, far))

    urgent.append(grid.swap_parity(tiles[2], on_group))
    send_raw(tiles, 1)
    columns, *turn = rotation_of(
        jnp.where(is_first, packed, other),
        jnp.where(is_first, other, packed),
        grid.row_high,
        0,
        grid.parity,
    )
    tiles, columns, turn, urgent, far = gate((tiles, columns, turn, urgent, far))

    arrived = grid.swap_row_high(columns, on_group)
    urgent += [grid.swap_parity(tiles[k], on_group) for k in range(3, count)]
    send_raw(tiles, 1)
    columns = jnp.stack((jnp.where(same, columns, arrived), jnp.where(same, arrived, columns)))
    tiles, columns, turn, urgent, far = gate((tiles, columns, turn, urgent, far))

    columns = grid.spread_row_group(columns)
    near_weights = weights_of(columns[0], grid.parity)
    far_weights = weights_of(columns[1], grid.parity)
    partner = [[urgent[k]] for k in range(count)]
    if groups:
        for k in late:
            partner[k].append(grid.swap_parity(tiles[k], off_group))
    send_raw(tiles, 2)
    block_turn = [rows_of(part, grid.parity ^ grid.row_high, width) for part in turn]
    blocks = jnp.stack(
        [
            rotate([[tiles[k]]], [[urgent[k]]], *near_weights, block_turn)[0]
            for k in range(count)
        ]
    )
    state = (tiles, near_weights, far_weights, partner, far, blocks, turn)
    tiles, near_weights, far_weights, partner, far, blocks, turn = gate(state)

    near, sent = {}, {}

    def first_round(k):
        near[k], sent[k] = rotate([[tiles[k]]], [partner[k]], *near_weights, turn)

    own_centres = diagonal(blocks)
    row_centres = grid.swap_col_high(own_centres, on_pair)
    col_centres = grid.swap_row_high(own_centres, on_pair)
    if groups:
        partner[early[0]].append(grid.swap_parity(tiles[early[0]], off_group))
    send_raw(tiles, len(raw_queue))
    first_round(late[0])
    own = second_generator(grid, blocks, own_centres, row_centres, col_centres)
    tiles, partner, far, own, near, sent = gate((tiles, partner, far, own, near, sent))

    late_near = cut(near[late[0]], block)
    late_far = {k: [] for k in late}
    other = grid.swap_row_high(own, on_group)
    if groups:
        for k in early[1:]:
            partner[k].append(grid.swap_parity(tiles[k], off_group))
    late_far[late[0]].append(grid.swap_col_high(late_near[0]))
    first_round(late[1])
    top, bottom = jnp.where(is_low, own, other), jnp.where(is_low, other, own)
    row, col = triangle_masks(width)
    packed = jnp.where(
        is_left, jnp.where(row < col, top, bottom), jnp.where(row < col, bottom, top)
    )
    state = (tiles, partner, near, sent, packed, late_far, late_near)
    tiles, partner, near, sent, packed, late_far, late_near = gate(state)

    arrived = grid.swap_parity(packed, lambda rh, rg, ch, cg, e: rg == cg and e == rh)
    late_far[late[0]] += [grid.swap_col_high(part) for part in late_near[1:]]
    moved = {late[0]: grid.swap_row_high(sent[late[0]])}
    first_round(early[0])
    packed = jnp.where(grid.parity == grid.row_high, packed, arrived)
    state = (tiles, partner, near, sent, packed, late_far, moved, far)
    tiles, partner, near, sent, packed, late_far, moved, far = gate(state)

    raw_pieces = [(k, piece) for k in early for piece in range(pieces_of)]
    far_partner = {k: [] for k in early}

    def send_far(number):
        for k, piece in take(raw_pieces, number):
            far_partner[k].append(grid.swap_parity(far[k][piece]))

    other = grid.swap_col_high(packed, on_group)
    moved[late[1]] = grid.swap_row_high(sent[late[1]])
    first_round(early[1])
    send_far(2)
    both = jnp.stack((jnp.where(is_left, packed, other), jnp.where(is_left, other, packed)))
    state = (near, sent, both, late_far, moved, far, far_partner)
    near, sent, both, late_far, moved, far, far_partner = gate(state)

    both = grid.spread_col_group(both)
    moved[early[0]] = grid.swap_row_high(sent[early[0]])
    late_near = cut(moved[late[0]], block)
    late_far[late[0]].append(grid.swap_col_high(late_near[0]))
    send_far(2)
    state = (sent, both, late_far, late_near, moved, far, far_partner)
    sent, both, late_far, late_near, moved, far, far_partner = gate(state)

    moved[early[1]] = grid.swap_row_high(sent[early[1]])
    late_far[late[0]] += [grid.swap_col_high(part) for part in late_near[1:]]
    send_far(2)
    columns, *second_turn = rotation_of(
        both[0], both[1], grid.row_high, grid.row_high, grid.col_high
    )
    state = (near, columns, second_turn, late_far, moved, far, far_partner)
    near, columns, second_turn, late_far, moved, far, far_partner = gate(state)

    def far_round(k):
        pieces = [[part] for part in far[k]]
        others = [[part] for part in far_partner[k]]
        return rotate(pieces, others, *far_weights, turn)

    arrived = grid.swap_row_high(columns, lambda rh, rg, ch, cg, e: rg == cg and rh == e)
    late_near = cut(near[late[1]], block)
    late_far[late[1]].append(grid.swap_col_high(late_near[0]))
    send_far(len(raw_pieces))
    far_near, far_sent = {}, {}
    far_near[early[0]], far_sent[early[0]] = far_round(early[0])
    columns = jnp.where(grid.row_high == grid.parity, columns, arrived)
    state = (columns, late_far, late_near, moved, far_near, far_sent, far_partner)
    columns, late_far, late_near, moved, far_near, far_sent, far_partner = gate(state)

    columns = grid.spread_row_group(columns)
    late_far[late[1]] += [grid.swap_col_high(part) for part in late_near[1:]]
    far_moved = {early[0]: grid.swap_row_high(far_sent[early[0]])}
    far_near[early[1]], far_sent[early[1]] = far_round(early[1])
    weights = weights_of(columns, grid.col_high)
    state = (weights, late_far, moved, far_near, far_sent, far_moved)
    weights, late_far, moved, far_near, far_sent, far_moved = gate(state)

    late_far[late[1]] += [grid.swap_col_high(part) for part in cut(moved[late[1]], block)]
    far_moved[early[1]] = grid.swap_row_high(far_sent[early[1]])
    outputs = [None] * count
    for k in [late[0], *early, late[1]]:
        mine = [[near[k]], [moved[k]]]
        if k in early:
            theirs = [[far_near[k]], [far_moved[k]]]
        else:
            theirs = [[part] for part in late_far[k]]
        kept, leaving = rotate(mine, theirs, *weights, second_turn)
        arrived = grid.swap_row_high(leaving)
        outputs[k] = [jnp.where(is_low, kept, arrived), jnp.where(is_low, arrived, kept)]
    return jnp.stack([part for pair in outputs for part in pair]).reshape(positions.shape)


def solution(mesh):
    spec = P(None, "row", "col")
    return jax.shard_map(local, mesh=mesh, in_specs=(spec,), out_specs=spec, check_vma=False)
```

```python
import functools

import jax
import jax.numpy as jnp
from jax import lax
from jax.experimental import pallas as pl
from jax.experimental.pallas import tpu as pltpu
from jax.sharding import PartitionSpec as P

STEP_SIZE = 0.4


def after(value, *earlier):
    return lax.optimization_barrier((value, *earlier))[0]


class Grid:
    def __init__(self, rows, cols):
        self.rows, self.cols = rows, cols
        self.groups = rows // 2
        row_id, col_id = lax.axis_index("row"), lax.axis_index("col")
        self.row_high, self.row_group = row_id // self.groups, row_id % self.groups
        self.col_high = col_id // (cols // 2)
        self.col_group = col_id % (cols // 2) // 2
        self.parity = col_id % 2

    def split(self, row, col):
        half = self.cols // 2
        return row // self.groups, row % self.groups, col // half, col % half // 2, col % 2

    def send(self, value, row_flip, col_flip, chosen=None):
        pairs = []
        for row in range(self.rows):
            for col in range(self.cols):
                if chosen is None or chosen(*self.split(row, col)):
                    target = (row ^ row_flip) * self.cols + (col ^ col_flip)
                    pairs.append((row * self.cols + col, target))
        return lax.ppermute(value, ("row", "col"), pairs)

    def swap_parity(self, value, chosen=None):
        return self.send(value, 0, 1, chosen)

    def swap_col_high(self, value, chosen=None):
        return self.send(value, 0, self.cols // 2, chosen)

    def swap_row_high(self, value, chosen=None):
        return self.send(value, self.rows // 2, 0, chosen)

    def spread_col_group(self, value):
        bit = 1
        while bit < self.groups:
            def holds(rh, rg, ch, cg, e, bit=bit):
                return (rg ^ cg) < bit

            arrived = self.send(value, 0, 2 * bit, holds)
            value = jnp.where((self.row_group ^ self.col_group) & bit != 0, arrived, value)
            bit *= 2
        return value

    def spread_row_group(self, value):
        bit = 1
        while bit < self.groups:
            def holds(rh, rg, ch, cg, e, bit=bit):
                return (rg ^ cg) < bit

            arrived = self.send(value, bit, 0, holds)
            value = jnp.where((self.row_group ^ self.col_group) & bit != 0, arrived, value)
            bit *= 2
        return value


def on_group(rh, rg, ch, cg, e):
    return rg == cg


def off_group(rh, rg, ch, cg, e):
    return rg != cg


def on_pair(rh, rg, ch, cg, e):
    return rg == cg and rh == ch


def triangle_masks(width):
    row = lax.broadcasted_iota(jnp.int32, (width, width), 0)
    col = lax.broadcasted_iota(jnp.int32, (width, width), 1)
    return row, col


def diagonal(blocks):
    row, col = triangle_masks(blocks.shape[-1])
    return jnp.sum(jnp.where((row == col)[None], blocks, 0.0), axis=1)


def halves(value):
    high = value.astype(jnp.bfloat16)
    return high, (value - high.astype(jnp.float32)).astype(jnp.bfloat16)


def beside(high, low):
    return jnp.concatenate((high, low, high), axis=1)


def stack_parts(ref, row, value):
    rows = value.shape[0]
    high, low = halves(value)
    stride = ref.shape[0] // 3
    for part, kept in enumerate((high, high, low)):
        ref[pl.ds(row + part * stride, rows), :] = kept


def dot(left, right):
    return jnp.dot(left, right, preferred_element_type=jnp.float32)


def rotation_kernel(
    flags_ref, first_ref, second_ref, columns_ref, high_ref, low_ref,
    gen, square_ref, gen_parts, in_parts,
):
    width = first_ref.shape[0]
    size = 2 * width
    step = min(width, 256)
    first, second = first_ref[...], second_ref[...]
    first_t, second_t = first.T, second.T
    row, col = triangle_masks(width)
    gen[:width, :width] = jnp.where(row < col, first, jnp.where(row > col, -first_t, 0.0))
    gen[width:, width:] = jnp.where(row < col, second, jnp.where(row > col, -second_t, 0.0))
    gen[width:, :width] = jnp.where(row >= col, first, -second_t)
    gen[:width, width:] = jnp.where(row <= col, -first_t, second)
    for start in range(0, size, step):
        stack_parts(gen_parts, start, gen[start : start + step, :])

    def on_eye(index):
        row = lax.broadcasted_iota(jnp.int32, (step, size), 0) + index * step
        return row == lax.broadcasted_iota(jnp.int32, (step, size), 1)

    def square(index, carry):
        rows = pl.ds(pl.multiple_of(index * step, step), step)
        start = index * step
        high = gen_parts[pl.ds(pl.multiple_of(start, step), step), :]
        low = gen_parts[pl.ds(pl.multiple_of(start + 2 * size, step), step), :]
        product = dot(beside(high, low), gen_parts[...])
        square_ref[rows, :] = product
        value = gen[rows, :] * (1 / 6) + product * (1 / 24)
        value = value + jnp.where(on_eye(index), 0.5, 0.0)
        stack_parts(in_parts, pl.multiple_of(start, step), value)
        return carry

    lax.fori_loop(0, size // step, square, 0)
    swap_rows, swap_cols, chosen = flags_ref[0], flags_ref[1], flags_ref[2]

    def outer(index, carry):
        rows = pl.ds(pl.multiple_of(index * step, step), step)
        product = dot(beside(*halves(square_ref[rows, :])), in_parts[...])
        value = product + gen[rows, :] + jnp.where(on_eye(index), 1.0, 0.0)
        columns_ref[rows, :] = jnp.where(chosen == 0, value[:, :width], value[:, width:])
        turned = value.T
        per_half = width // step
        place = (index // per_half + swap_cols) % 2 * per_half + index % per_half
        cols = pl.ds(pl.multiple_of(place * step, step), step)
        for part in range(2):
            start = pl.multiple_of((part + swap_rows) % 2 * width, width)
            high, low = halves(turned[part * width : (part + 1) * width])
            high_ref[pl.ds(start, width), cols] = high
            low_ref[pl.ds(start, width), cols] = low
        return carry

    lax.fori_loop(0, size // step, outer, 0)


NO_COST = pl.CostEstimate(flops=0, bytes_accessed=0, transcendentals=0)


def rotation_of(first, second, swap_rows, swap_cols, chosen):
    width = first.shape[0]
    size = 2 * width
    whole = pl.BlockSpec(memory_space=pltpu.VMEM)
    flags = jnp.stack([jnp.asarray(flag, jnp.int32) for flag in (swap_rows, swap_cols, chosen)])
    return pl.pallas_call(
        rotation_kernel,
        out_shape=(
            jax.ShapeDtypeStruct((size, width), jnp.float32),
            jax.ShapeDtypeStruct((size, size), jnp.bfloat16),
            jax.ShapeDtypeStruct((size, size), jnp.bfloat16),
        ),
        in_specs=[pl.BlockSpec(memory_space=pltpu.SMEM), whole, whole],
        out_specs=(whole, whole, whole),
        scratch_shapes=[pltpu.VMEM((size, size), jnp.float32)] * 2
        + [pltpu.VMEM((3 * size, size), jnp.bfloat16)] * 2,
        compiler_params=pltpu.CompilerParams(vmem_limit_bytes=48 * 2**20),
        cost_estimate=NO_COST,
    )(flags, first, second)


def rotate_kernel(spans, per_half, *refs):
    step = pl.program_id(0)
    at = sum(count for side in spans for _, _, count in side)
    weights, turn_high, turn_low = refs[at : at + 2], refs[at + 2], refs[at + 3]
    outs = refs[at + 4 : -3]
    weight_parts, mid_parts = refs[-3:-1], refs[-1]
    block = turn_high.shape[0]
    first_part = 2 * per_half

    @pl.when(step == 0)
    def _():
        for side in range(2):
            stack_parts(weight_parts[side], 0, weights[side][...])

    for now in range(first_part):

        @pl.when(step == now)
        def _(now=now):
            total, at = None, 0
            for side in range(2):
                for first, steps, count in spans[side]:
                    if first <= now < first + steps:
                        value = refs[at][...]
                        for ref in refs[at + 1 : at + count]:
                            value = value + ref[...]
                        part = dot(beside(*halves(value)), weight_parts[side][...])
                        total = part if total is None else total + part
                    at += count
            stack_parts(mid_parts, now * block, total)

    @pl.when(step >= first_part)
    def _():
        product = dot(beside(turn_high[...], turn_low[...]), mid_parts[...])
        for half, out in enumerate(outs):

            @pl.when((step - first_part) // per_half == half)
            def _(out=out):
                out[...] = product


def block_rows(width):
    return min(width, 256)


def rotate(near, far, near_weights, far_weights, turn):
    width = near_weights.shape[0]
    size = 2 * width
    block = block_rows(width)
    per_half = width // block
    first_part = 2 * per_half
    turn_high, turn_low = turn
    out_halves = turn_high.shape[0] // width
    arrays, specs, spans = [], [], []
    for side in (near, far):
        span, first = [], 0
        for piece in side:
            steps = piece[0].shape[0] // block
            span.append((first, steps, len(piece)))

            def place(step, first=first, steps=steps):
                return jnp.clip(step - first, 0, steps - 1), 0

            for array in piece:
                arrays.append(array)
                specs.append(pl.BlockSpec((block, width), place))
            first += steps
        spans.append(tuple(span))
    fixed = pl.BlockSpec((width, width), lambda step: (0, 0))
    turning = pl.BlockSpec(
        (block, size),
        lambda step: (jnp.clip(step - first_part, 0, out_halves * per_half - 1), 0),
    )
    outs = [
        pl.BlockSpec(
            (block, width),
            lambda step, half=half: (
                jnp.clip(step - first_part - half * per_half, 0, per_half - 1),
                0,
            ),
        )
        for half in range(out_halves)
    ]
    return pl.pallas_call(
        functools.partial(rotate_kernel, tuple(spans), per_half),
        grid=(first_part + out_halves * per_half,),
        out_shape=[jax.ShapeDtypeStruct((width, width), jnp.float32)] * out_halves,
        in_specs=[*specs, fixed, fixed, turning, turning],
        out_specs=outs,
        scratch_shapes=[pltpu.VMEM((3 * width, width), jnp.bfloat16)] * 2
        + [pltpu.VMEM((3 * size, width), jnp.bfloat16)],
        compiler_params=pltpu.CompilerParams(vmem_limit_bytes=40 * 2**20),
        cost_estimate=NO_COST,
    )(*arrays, near_weights, far_weights, turn_high, turn_low)


def rows_of(value, which, width):
    return lax.dynamic_slice_in_dim(value, which * width, width, value.ndim - 2)


def first_generator(grid, tiles, own_centres, other_centres):
    width = tiles.shape[2]
    is_first = grid.parity == 0
    centres = jnp.where(
        is_first,
        jnp.concatenate((own_centres, other_centres), axis=1),
        jnp.concatenate((other_centres, own_centres), axis=1),
    )
    generator = STEP_SIZE * jnp.sum(
        tiles * (own_centres[:, None, :] - centres[:, :, None]), axis=0
    )
    row, col = triangle_masks(width)
    top, bottom = generator[:width], generator[width:]
    return jnp.where(
        is_first, jnp.where(row < col, top, bottom), jnp.where(row < col, bottom, top)
    )


def second_generator(grid, blocks, own_centres, row_centres, col_centres):
    same = grid.row_high == grid.col_high
    row_centres = jnp.where(same, own_centres, row_centres)
    col_centres = jnp.where(same, own_centres, col_centres)
    return STEP_SIZE * jnp.sum(
        blocks * (col_centres[:, None, :] - row_centres[:, :, None]), axis=0
    )


def local(positions):
    grid = Grid(lax.axis_size("row"), lax.axis_size("col"))
    count, height, width = positions.shape
    half = count // 2
    block = block_rows(width)
    early, late = list(range(half)), list(range(half, count))
    is_first = grid.parity == 0
    is_low = grid.row_high == 0
    is_left = grid.col_high == 0
    same = grid.row_high == grid.col_high
    groups = grid.groups > 1

    def weights_of(columns, which):
        return rows_of(columns, which, width), rows_of(columns, 1 - which, width)

    raw_queue = [(k, row) for k in early for row in range(0, height, block)]
    raw = {k: [] for k in early}

    def send_raw(pieces, token):
        arrived = []
        for k, row in raw_queue[:pieces]:
            rows = after(positions[k, row : row + block], token)
            arrived.append(grid.swap_col_high(rows))
            raw[k].append(arrived[-1])
        del raw_queue[:pieces]
        return arrived

    urgent, rest = [None] * count, {}

    def send_urgent(k, *tokens):
        urgent[k] = grid.swap_parity(after(positions[k], *tokens), on_group)

    def send_rest(k, *tokens):
        rest[k] = grid.swap_parity(after(positions[k], *tokens), off_group) if groups else None

    def rests(k):
        return [rest[k]] if groups else []

    own_centres = diagonal(rows_of(positions, grid.parity, width))
    other_centres = grid.swap_parity(own_centres, on_pair)
    packed = first_generator(grid, positions, own_centres, other_centres)
    packed = jnp.where(same, packed, grid.swap_col_high(packed, on_pair))
    send_urgent(0, packed)
    pieces = []
    packed = grid.spread_col_group(packed)
    pieces_next = send_raw(1, packed)
    packed = after(packed, urgent[0], *pieces)
    other = after(grid.swap_parity(packed), *pieces_next)
    send_urgent(1, other)
    pieces = send_raw(1, other)
    columns, *turn = rotation_of(
        jnp.where(is_first, packed, other),
        jnp.where(is_first, other, packed),
        grid.row_high,
        0,
        grid.parity,
    )
    columns = after(columns, urgent[1], *pieces)
    send_urgent(2, columns)
    pieces = send_raw(2, columns)
    arrived = grid.swap_row_high(columns, on_group)
    columns = jnp.stack((jnp.where(same, columns, arrived), jnp.where(same, arrived, columns)))
    columns = after(columns, *pieces, urgent[2])
    send_urgent(3, columns)
    send_rest(late[0], columns)
    send_rest(late[1], columns)
    pieces = send_raw(2, columns)
    columns = grid.spread_row_group(columns)
    near_weights = weights_of(columns[0], grid.parity)
    far_weights = weights_of(columns[1], grid.parity)

    block_turn = [rows_of(part, grid.parity ^ grid.row_high, width) for part in turn]
    blocks = jnp.stack(
        [
            rotate([[positions[k]]], [[urgent[k]]], *near_weights, block_turn)[0]
            for k in range(count)
        ]
    )
    blocks = after(blocks, *pieces, *rests(late[0]))
    pieces = send_raw(len(raw_queue), blocks)
    send_rest(early[0], blocks)
    own_centres = diagonal(blocks)
    row_centres = grid.swap_col_high(own_centres, on_pair)
    col_centres = grid.swap_row_high(own_centres, on_pair)
    own = second_generator(grid, blocks, own_centres, row_centres, col_centres)
    other = grid.swap_row_high(own, lambda rh, rg, ch, cg, e: rg == cg and rh != e)

    near, sent, moved = {}, {}, {}

    def first_round(k, token):
        partner = [urgent[k], *rests(k)]
        tile = after(positions[k], token)
        near[k], sent[k] = rotate([[tile]], [partner], *near_weights, turn)

    def move(k, token):
        moved[k] = grid.swap_row_high(after(sent[k], token))

    away = grid.send(own, grid.rows // 2, 1, lambda rh, rg, ch, cg, e: rg == cg and rh != e)
    beside_own = grid.swap_parity(own, lambda rh, rg, ch, cg, e: rg == cg and rh == e)
    at_home = grid.parity == grid.row_high
    mine, theirs = jnp.where(at_home, own, beside_own), jnp.where(at_home, other, away)
    first_round(late[0], blocks)
    move(late[0], own)
    first_round(late[1], own)
    top, bottom = jnp.where(is_low, mine, theirs), jnp.where(is_low, theirs, mine)
    row, col = triangle_masks(width)
    packed = jnp.where(
        is_left, jnp.where(row < col, top, bottom), jnp.where(row < col, bottom, top)
    )
    packed = after(packed, near[late[1]], moved[late[0]], *pieces)
    packed = after(packed, *rests(early[0]))
    other = grid.swap_col_high(packed, on_group)
    move(late[1], packed)
    first_round(early[0], packed)
    move(early[0], packed)
    send_rest(early[1], packed)
    far_queue = [(k, part) for k in early for part in range(2)]
    far_partner = {k: [] for k in early}

    def send_far(token):
        k, part = far_queue.pop(0)
        pieces = raw[k][part * len(raw[k]) // 2 : (part + 1) * len(raw[k]) // 2]
        rows = jnp.concatenate(pieces, axis=0)
        far_partner[k].append(grid.swap_parity(after(rows, token)))
        return far_partner[k][-1]

    late_far = {k: [] for k in late}

    def send_late(k, part, token):
        late_far[k].append(grid.swap_col_high(after(part, token)))
        return late_far[k][-1]

    middle = width // 2
    pieces = [send_late(late[0], near[late[0]][:middle], packed)]
    partner = send_far(packed)
    both = jnp.stack((jnp.where(is_left, packed, other), jnp.where(is_left, other, packed)))
    both = after(both, moved[late[1]], moved[early[0]], *pieces, partner, *rests(early[1]))
    parts = (near[late[0]][middle:], moved[late[0]][:middle])
    late_half = send_late(late[0], jnp.concatenate(parts, axis=0), both)
    partner = [send_far(both), send_far(both)]
    first_round(early[1], both)
    move(early[1], both)
    both = grid.spread_col_group(both)
    both = after(both, moved[early[1]], *partner)
    far_near, far_sent, far_moved = {}, {}, {}

    def far_round(k, token):
        tiles = [[after(part, token)] for part in raw[k]]
        others = [[part] for part in far_partner[k]]
        far_near[k], far_sent[k] = rotate(tiles, others, *far_weights, turn)

    late_quarter = send_late(late[0], moved[late[0]][middle:], both)
    partner = send_far(both)
    columns, *second_turn = rotation_of(
        both[0], both[1], grid.row_high, grid.row_high, grid.col_high
    )
    columns = after(columns, late_half, partner)
    far_round(early[0], columns)
    far_round(early[1], columns)
    arrived = grid.swap_row_high(columns, lambda rh, rg, ch, cg, e: rg == cg and rh == e)
    columns = jnp.where(grid.row_high == grid.parity, columns, arrived)
    far_moved[early[0]] = grid.swap_row_high(far_sent[early[0]])
    columns = after(columns, far_near[early[0]], far_near[early[1]], late_quarter)
    far_moved[early[1]] = grid.swap_row_high(after(far_sent[early[1]], columns))
    for part in (near[late[1]], moved[late[1]]):
        send_late(late[1], part, columns)
    weights = weights_of(grid.spread_row_group(columns), grid.col_high)
    weights = [after(weight, far_moved[early[0]]) for weight in weights]

    outputs = [None] * count
    before = [late_far[late[1]][0]]
    for k in [*early, *late]:
        mine = [[near[k]], [moved[k]]]
        theirs = [[far_near[k]], [far_moved[k]]] if k in early else [[part] for part in late_far[k]]
        kept, leaving = rotate(mine, theirs, *weights, second_turn)
        arrived = grid.swap_row_high(leaving)
        if k == late[0]:
            before.append(arrived)
        weights = [after(weight, kept, *before) for weight in weights]
        before = [arrived]
        outputs[k] = [jnp.where(is_low, kept, arrived), jnp.where(is_low, arrived, kept)]
    return jnp.stack([part for pair in outputs for part in pair]).reshape(positions.shape)


def solution(mesh):
    spec = P(None, "row", "col")
    return jax.shard_map(local, mesh=mesh, in_specs=(spec,), out_specs=spec, check_vma=False)
```

```python
import functools

import jax
import jax.numpy as jnp
from jax import lax
from jax.experimental import pallas as pl
from jax.experimental.pallas import tpu as pltpu
from jax.sharding import PartitionSpec as P

STEP_SIZE = 0.4


def after(value, *earlier):
    return lax.optimization_barrier((value, *earlier))[0]


class Grid:
    def __init__(self, rows, cols):
        self.rows, self.cols = rows, cols
        self.groups = rows // 2
        row_id, col_id = lax.axis_index("row"), lax.axis_index("col")
        self.row_high, self.row_group = row_id // self.groups, row_id % self.groups
        self.col_high = col_id // (cols // 2)
        self.col_group = col_id % (cols // 2) // 2
        self.parity = col_id % 2

    def split(self, row, col):
        half = self.cols // 2
        return row // self.groups, row % self.groups, col // half, col % half // 2, col % 2

    def send(self, value, row_flip, col_flip, chosen=None):
        pairs = []
        for row in range(self.rows):
            for col in range(self.cols):
                if chosen is None or chosen(*self.split(row, col)):
                    target = (row ^ row_flip) * self.cols + (col ^ col_flip)
                    pairs.append((row * self.cols + col, target))
        return lax.ppermute(value, ("row", "col"), pairs)

    def swap_parity(self, value, chosen=None):
        return self.send(value, 0, 1, chosen)

    def swap_col_high(self, value, chosen=None):
        return self.send(value, 0, self.cols // 2, chosen)

    def swap_row_high(self, value, chosen=None):
        return self.send(value, self.rows // 2, 0, chosen)

    def spread_col_group(self, value):
        bit = 1
        while bit < self.groups:
            def holds(rh, rg, ch, cg, e, bit=bit):
                return (rg ^ cg) < bit

            arrived = self.send(value, 0, 2 * bit, holds)
            value = jnp.where((self.row_group ^ self.col_group) & bit != 0, arrived, value)
            bit *= 2
        return value

    def spread_row_group(self, value):
        bit = 1
        while bit < self.groups:
            def holds(rh, rg, ch, cg, e, bit=bit):
                return (rg ^ cg) < bit

            arrived = self.send(value, bit, 0, holds)
            value = jnp.where((self.row_group ^ self.col_group) & bit != 0, arrived, value)
            bit *= 2
        return value


def on_group(rh, rg, ch, cg, e):
    return rg == cg


def off_group(rh, rg, ch, cg, e):
    return rg != cg


def on_pair(rh, rg, ch, cg, e):
    return rg == cg and rh == ch


def triangle_masks(width):
    row = lax.broadcasted_iota(jnp.int32, (width, width), 0)
    col = lax.broadcasted_iota(jnp.int32, (width, width), 1)
    return row, col


def diagonal(blocks):
    row, col = triangle_masks(blocks.shape[-1])
    return jnp.sum(jnp.where((row == col)[None], blocks, 0.0), axis=1)


def halves(value):
    high = value.astype(jnp.bfloat16)
    return high, (value - high.astype(jnp.float32)).astype(jnp.bfloat16)


def beside(high, low):
    return jnp.concatenate((high, low, high), axis=1)


def stack_parts(ref, row, value):
    rows = value.shape[0]
    high, low = halves(value)
    stride = ref.shape[0] // 3
    for part, kept in enumerate((high, high, low)):
        ref[pl.ds(row + part * stride, rows), :] = kept


def dot(left, right):
    return jnp.dot(left, right, preferred_element_type=jnp.float32)


def rotation_kernel(
    flags_ref, first_ref, second_ref, columns_ref, high_ref, low_ref,
    gen, square_ref, gen_parts, in_parts,
):
    width = first_ref.shape[0]
    size = 2 * width
    step = min(width, 256)
    first, second = first_ref[...], second_ref[...]
    first_t, second_t = first.T, second.T
    row, col = triangle_masks(width)
    gen[:width, :width] = jnp.where(row < col, first, jnp.where(row > col, -first_t, 0.0))
    gen[width:, width:] = jnp.where(row < col, second, jnp.where(row > col, -second_t, 0.0))
    gen[width:, :width] = jnp.where(row >= col, first, -second_t)
    gen[:width, width:] = jnp.where(row <= col, -first_t, second)
    for start in range(0, size, step):
        stack_parts(gen_parts, start, gen[start : start + step, :])

    def on_eye(index):
        row = lax.broadcasted_iota(jnp.int32, (step, size), 0) + index * step
        return row == lax.broadcasted_iota(jnp.int32, (step, size), 1)

    def square(index, carry):
        rows = pl.ds(pl.multiple_of(index * step, step), step)
        start = index * step
        high = gen_parts[pl.ds(pl.multiple_of(start, step), step), :]
        low = gen_parts[pl.ds(pl.multiple_of(start + 2 * size, step), step), :]
        product = dot(beside(high, low), gen_parts[...])
        square_ref[rows, :] = product
        value = gen[rows, :] * (1 / 6) + product * (1 / 24)
        value = value + jnp.where(on_eye(index), 0.5, 0.0)
        stack_parts(in_parts, pl.multiple_of(start, step), value)
        return carry

    lax.fori_loop(0, size // step, square, 0)
    swap_rows, swap_cols, chosen = flags_ref[0], flags_ref[1], flags_ref[2]

    def outer(index, carry):
        rows = pl.ds(pl.multiple_of(index * step, step), step)
        product = dot(beside(*halves(square_ref[rows, :])), in_parts[...])
        value = product + gen[rows, :] + jnp.where(on_eye(index), 1.0, 0.0)
        columns_ref[rows, :] = jnp.where(chosen == 0, value[:, :width], value[:, width:])
        turned = value.T
        per_half = width // step
        place = (index // per_half + swap_cols) % 2 * per_half + index % per_half
        cols = pl.ds(pl.multiple_of(place * step, step), step)
        for part in range(2):
            start = pl.multiple_of((part + swap_rows) % 2 * width, width)
            high, low = halves(turned[part * width : (part + 1) * width])
            high_ref[pl.ds(start, width), cols] = high
            low_ref[pl.ds(start, width), cols] = low
        return carry

    lax.fori_loop(0, size // step, outer, 0)


NO_COST = pl.CostEstimate(flops=0, bytes_accessed=0, transcendentals=0)


def rotation_of(first, second, swap_rows, swap_cols, chosen):
    width = first.shape[0]
    size = 2 * width
    whole = pl.BlockSpec(memory_space=pltpu.VMEM)
    flags = jnp.stack([jnp.asarray(flag, jnp.int32) for flag in (swap_rows, swap_cols, chosen)])
    return pl.pallas_call(
        rotation_kernel,
        out_shape=(
            jax.ShapeDtypeStruct((size, width), jnp.float32),
            jax.ShapeDtypeStruct((size, size), jnp.bfloat16),
            jax.ShapeDtypeStruct((size, size), jnp.bfloat16),
        ),
        in_specs=[pl.BlockSpec(memory_space=pltpu.SMEM), whole, whole],
        out_specs=(whole, whole, whole),
        scratch_shapes=[pltpu.VMEM((size, size), jnp.float32)] * 2
        + [pltpu.VMEM((3 * size, size), jnp.bfloat16)] * 2,
        compiler_params=pltpu.CompilerParams(vmem_limit_bytes=48 * 2**20),
        cost_estimate=NO_COST,
    )(flags, first, second)


def rotate_kernel(spans, per_half, *refs):
    step = pl.program_id(0)
    at = sum(count for side in spans for _, _, count in side)
    weights, turn_high, turn_low = refs[at : at + 2], refs[at + 2], refs[at + 3]
    outs = refs[at + 4 : -3]
    weight_parts, mid_parts = refs[-3:-1], refs[-1]
    block = turn_high.shape[0]
    first_part = 2 * per_half

    @pl.when(step == 0)
    def _():
        for side in range(2):
            stack_parts(weight_parts[side], 0, weights[side][...])

    for now in range(first_part):

        @pl.when(step == now)
        def _(now=now):
            total, at = None, 0
            for side in range(2):
                for first, steps, count in spans[side]:
                    if first <= now < first + steps:
                        value = refs[at][...]
                        for ref in refs[at + 1 : at + count]:
                            value = value + ref[...]
                        part = dot(beside(*halves(value)), weight_parts[side][...])
                        total = part if total is None else total + part
                    at += count
            stack_parts(mid_parts, now * block, total)

    @pl.when(step >= first_part)
    def _():
        product = dot(beside(turn_high[...], turn_low[...]), mid_parts[...])
        for half, out in enumerate(outs):

            @pl.when((step - first_part) // per_half == half)
            def _(out=out):
                out[...] = product


def block_rows(width):
    return min(width, 256)


def rotate(near, far, near_weights, far_weights, turn):
    width = near_weights.shape[0]
    size = 2 * width
    block = block_rows(width)
    per_half = width // block
    first_part = 2 * per_half
    turn_high, turn_low = turn
    out_halves = turn_high.shape[0] // width
    arrays, specs, spans = [], [], []
    for side in (near, far):
        span, first = [], 0
        for piece in side:
            steps = piece[0].shape[0] // block
            span.append((first, steps, len(piece)))

            def place(step, first=first, steps=steps):
                return jnp.clip(step - first, 0, steps - 1), 0

            for array in piece:
                arrays.append(array)
                specs.append(pl.BlockSpec((block, width), place))
            first += steps
        spans.append(tuple(span))
    fixed = pl.BlockSpec((width, width), lambda step: (0, 0))
    turning = pl.BlockSpec(
        (block, size),
        lambda step: (jnp.clip(step - first_part, 0, out_halves * per_half - 1), 0),
    )
    outs = [
        pl.BlockSpec(
            (block, width),
            lambda step, half=half: (
                jnp.clip(step - first_part - half * per_half, 0, per_half - 1),
                0,
            ),
        )
        for half in range(out_halves)
    ]
    return pl.pallas_call(
        functools.partial(rotate_kernel, tuple(spans), per_half),
        grid=(first_part + out_halves * per_half,),
        out_shape=[jax.ShapeDtypeStruct((width, width), jnp.float32)] * out_halves,
        in_specs=[*specs, fixed, fixed, turning, turning],
        out_specs=outs,
        scratch_shapes=[pltpu.VMEM((3 * width, width), jnp.bfloat16)] * 2
        + [pltpu.VMEM((3 * size, width), jnp.bfloat16)],
        compiler_params=pltpu.CompilerParams(vmem_limit_bytes=40 * 2**20),
        cost_estimate=NO_COST,
    )(*arrays, near_weights, far_weights, turn_high, turn_low)


def rows_of(value, which, width):
    return lax.dynamic_slice_in_dim(value, which * width, width, value.ndim - 2)


def first_generator(grid, tiles, own_centres, other_centres):
    width = tiles.shape[2]
    is_first = grid.parity == 0
    centres = jnp.where(
        is_first,
        jnp.concatenate((own_centres, other_centres), axis=1),
        jnp.concatenate((other_centres, own_centres), axis=1),
    )
    generator = STEP_SIZE * jnp.sum(
        tiles * (own_centres[:, None, :] - centres[:, :, None]), axis=0
    )
    row, col = triangle_masks(width)
    top, bottom = generator[:width], generator[width:]
    return jnp.where(
        is_first, jnp.where(row < col, top, bottom), jnp.where(row < col, bottom, top)
    )


def second_generator(grid, blocks, own_centres, row_centres, col_centres):
    same = grid.row_high == grid.col_high
    row_centres = jnp.where(same, own_centres, row_centres)
    col_centres = jnp.where(same, own_centres, col_centres)
    return STEP_SIZE * jnp.sum(
        blocks * (col_centres[:, None, :] - row_centres[:, :, None]), axis=0
    )


def local(positions):
    grid = Grid(lax.axis_size("row"), lax.axis_size("col"))
    count, height, width = positions.shape
    half = count // 2
    block = block_rows(width)
    early, late = list(range(half)), list(range(half, count))
    is_first = grid.parity == 0
    is_low = grid.row_high == 0
    is_left = grid.col_high == 0
    same = grid.row_high == grid.col_high
    groups = grid.groups > 1

    def weights_of(columns, which):
        return rows_of(columns, which, width), rows_of(columns, 1 - which, width)

    raw_queue = [(k, row) for k in early for row in range(0, height, block)]
    raw = {k: [] for k in early}

    def send_raw(pieces, token):
        arrived = []
        for k, row in raw_queue[:pieces]:
            rows = after(positions[k, row : row + block], token)
            arrived.append(grid.swap_col_high(rows))
            raw[k].append(arrived[-1])
        del raw_queue[:pieces]
        return arrived

    urgent, rest = [None] * count, {}

    def send_urgent(k, *tokens):
        urgent[k] = grid.swap_parity(after(positions[k], *tokens), on_group)

    def send_rest(k, *tokens):
        rest[k] = grid.swap_parity(after(positions[k], *tokens), off_group) if groups else None

    def rests(k):
        return [rest[k]] if groups else []

    own_centres = diagonal(rows_of(positions, grid.parity, width))
    other_centres = grid.swap_parity(own_centres, on_pair)
    packed = first_generator(grid, positions, own_centres, other_centres)
    send_rest(late[0], other_centres)
    packed = jnp.where(same, packed, grid.swap_col_high(packed, on_pair))
    packed = after(packed, *rests(late[0]))
    send_rest(late[1], packed)
    packed = grid.spread_col_group(packed)
    packed = after(packed, *rests(late[1]))
    pieces = send_raw(1, packed)
    other = after(grid.swap_parity(packed), *pieces)
    send_urgent(0, other)
    pieces = send_raw(1, other)
    columns, *turn = rotation_of(
        jnp.where(is_first, packed, other),
        jnp.where(is_first, other, packed),
        grid.row_high,
        0,
        grid.parity,
    )
    columns = after(columns, urgent[0], *pieces)
    send_urgent(1, columns)
    send_rest(early[0], columns)
    pieces = send_raw(2, columns)
    arrived = grid.swap_row_high(columns, on_group)
    columns = jnp.stack((jnp.where(same, columns, arrived), jnp.where(same, arrived, columns)))
    columns = after(columns, *pieces, urgent[1], *rests(early[0]))
    send_urgent(2, columns)
    send_urgent(3, columns)
    pieces = send_raw(2, columns)
    columns = grid.spread_row_group(columns)
    near_weights = weights_of(columns[0], grid.parity)
    far_weights = weights_of(columns[1], grid.parity)

    block_turn = [rows_of(part, grid.parity ^ grid.row_high, width) for part in turn]
    blocks = jnp.stack(
        [
            rotate([[positions[k]]], [[urgent[k]]], *near_weights, block_turn)[0]
            for k in range(count)
        ]
    )
    blocks = after(blocks, *pieces)
    pieces = send_raw(len(raw_queue), blocks)
    send_rest(early[1], blocks)
    own_centres = diagonal(blocks)
    row_centres = grid.swap_col_high(own_centres, on_pair)
    col_centres = grid.swap_row_high(own_centres, on_pair)
    own = second_generator(grid, blocks, own_centres, row_centres, col_centres)
    other = grid.swap_row_high(own, lambda rh, rg, ch, cg, e: rg == cg and rh != e)

    near, sent, moved = {}, {}, {}

    def first_round(k, token):
        partner = [urgent[k], *rests(k)]
        tile = after(positions[k], token)
        near[k], sent[k] = rotate([[tile]], [partner], *near_weights, turn)

    def move(k, token):
        moved[k] = grid.swap_row_high(after(sent[k], token))

    away = grid.send(own, grid.rows // 2, 1, lambda rh, rg, ch, cg, e: rg == cg and rh != e)
    beside_own = grid.swap_parity(own, lambda rh, rg, ch, cg, e: rg == cg and rh == e)
    at_home = grid.parity == grid.row_high
    mine, theirs = jnp.where(at_home, own, beside_own), jnp.where(at_home, other, away)
    first_round(late[0], blocks)
    move(late[0], own)
    first_round(late[1], own)
    top, bottom = jnp.where(is_low, mine, theirs), jnp.where(is_low, theirs, mine)
    row, col = triangle_masks(width)
    packed = jnp.where(
        is_left, jnp.where(row < col, top, bottom), jnp.where(row < col, bottom, top)
    )
    packed = after(packed, near[late[1]], moved[late[0]], *pieces)
    packed = after(packed, *rests(early[1]))
    other = grid.swap_col_high(packed, on_group)
    move(late[1], packed)
    first_round(early[0], packed)
    move(early[0], packed)
    first_round(early[1], packed)
    far_queue = [(k, part) for k in early for part in range(2)]
    far_partner = {k: [] for k in early}

    def send_far(token):
        k, part = far_queue.pop(0)
        pieces = raw[k][part * len(raw[k]) // 2 : (part + 1) * len(raw[k]) // 2]
        rows = jnp.concatenate(pieces, axis=0)
        far_partner[k].append(grid.swap_parity(after(rows, token)))
        return far_partner[k][-1]

    late_far = {k: [] for k in late}

    def send_late(k, part, token):
        late_far[k].append(grid.swap_col_high(after(part, token)))
        return late_far[k][-1]

    middle = width // 2
    pieces = [send_late(late[0], near[late[0]][:middle], packed)]
    partner = [send_far(packed), send_far(packed)]
    both = jnp.stack((jnp.where(is_left, packed, other), jnp.where(is_left, other, packed)))
    both = after(both, moved[late[1]], moved[early[0]], near[early[1]], *pieces, *partner)
    parts = (near[late[0]][middle:], moved[late[0]][:middle])
    late_half = send_late(late[0], jnp.concatenate(parts, axis=0), both)
    partner = send_far(both)
    move(early[1], both)
    far_near, far_sent, far_moved = {}, {}, {}

    def far_round(k, token):
        tiles = [[after(part, token)] for part in raw[k]]
        others = [[part] for part in far_partner[k]]
        far_near[k], far_sent[k] = rotate(tiles, others, *far_weights, turn)

    def far_move(k, token):
        far_moved[k] = grid.swap_row_high(after(far_sent[k], token))

    far_round(early[0], both)
    both = grid.spread_col_group(both)
    both = after(both, far_near[early[0]], moved[early[1]], partner)
    late_quarter = send_late(late[0], moved[late[0]][middle:], both)
    far_move(early[0], both)
    partner = send_far(both)
    columns, *second_turn = rotation_of(
        both[0], both[1], grid.row_high, grid.row_high, grid.col_high
    )
    columns = after(columns, far_moved[early[0]], late_half, partner)
    far_round(early[1], columns)
    arrived = grid.swap_row_high(columns, lambda rh, rg, ch, cg, e: rg == cg and rh == e)
    columns = jnp.where(grid.row_high == grid.parity, columns, arrived)
    columns = after(columns, far_near[early[1]], late_quarter)
    far_move(early[1], columns)
    send_late(late[1], jnp.concatenate((near[late[1]], moved[late[1]]), axis=0), columns)
    weights = weights_of(grid.spread_row_group(columns), grid.col_high)

    outputs = [None] * count
    before = [far_moved[early[1]]]
    for k in [*early, *late]:
        mine = [[near[k]], [moved[k]]]
        theirs = [[far_near[k]], [far_moved[k]]] if k in early else [[part] for part in late_far[k]]
        kept, leaving = rotate(mine, theirs, *weights, second_turn)
        arrived = grid.swap_row_high(leaving)
        if k == late[0]:
            before.append(arrived)
        weights = [after(weight, kept, *before) for weight in weights]
        before = [arrived]
        outputs[k] = [jnp.where(is_low, kept, arrived), jnp.where(is_low, arrived, kept)]
    return jnp.stack([part for pair in outputs for part in pair]).reshape(positions.shape)


def solution(mesh):
    spec = P(None, "row", "col")
    return jax.shard_map(local, mesh=mesh, in_specs=(spec,), out_specs=spec, check_vma=False)
```

```python
import functools

import jax
import jax.numpy as jnp
from jax import lax
from jax.experimental import pallas as pl
from jax.experimental.pallas import tpu as pltpu
from jax.sharding import PartitionSpec as P

STEP_SIZE = 0.4


def after(value, *earlier):
    return lax.optimization_barrier((value, *earlier))[0]


class Grid:
    def __init__(self, rows, cols):
        self.rows, self.cols = rows, cols
        self.groups = rows // 2
        row_id, col_id = lax.axis_index("row"), lax.axis_index("col")
        self.row_high, self.row_group = row_id // self.groups, row_id % self.groups
        self.col_high = col_id // (cols // 2)
        self.col_group = col_id % (cols // 2) // 2
        self.parity = col_id % 2

    def split(self, row, col):
        half = self.cols // 2
        return row // self.groups, row % self.groups, col // half, col % half // 2, col % 2

    def send(self, value, row_flip, col_flip, chosen=None):
        pairs = []
        for row in range(self.rows):
            for col in range(self.cols):
                if chosen is None or chosen(*self.split(row, col)):
                    target = (row ^ row_flip) * self.cols + (col ^ col_flip)
                    pairs.append((row * self.cols + col, target))
        return lax.ppermute(value, ("row", "col"), pairs)

    def swap_parity(self, value, chosen=None):
        return self.send(value, 0, 1, chosen)

    def swap_col_high(self, value, chosen=None):
        return self.send(value, 0, self.cols // 2, chosen)

    def swap_row_high(self, value, chosen=None):
        return self.send(value, self.rows // 2, 0, chosen)

    def spread_col_group(self, value):
        bit = 1
        while bit < self.groups:
            def holds(rh, rg, ch, cg, e, bit=bit):
                return (rg ^ cg) < bit

            arrived = self.send(value, 0, 2 * bit, holds)
            value = jnp.where((self.row_group ^ self.col_group) & bit != 0, arrived, value)
            bit *= 2
        return value

    def spread_row_group(self, value):
        bit = 1
        while bit < self.groups:
            def holds(rh, rg, ch, cg, e, bit=bit):
                return (rg ^ cg) < bit

            arrived = self.send(value, bit, 0, holds)
            value = jnp.where((self.row_group ^ self.col_group) & bit != 0, arrived, value)
            bit *= 2
        return value


def on_group(rh, rg, ch, cg, e):
    return rg == cg


def off_group(rh, rg, ch, cg, e):
    return rg != cg


def on_pair(rh, rg, ch, cg, e):
    return rg == cg and rh == ch


def triangle_masks(width):
    row = lax.broadcasted_iota(jnp.int32, (width, width), 0)
    col = lax.broadcasted_iota(jnp.int32, (width, width), 1)
    return row, col


def diagonal(blocks):
    row, col = triangle_masks(blocks.shape[-1])
    return jnp.sum(jnp.where((row == col)[None], blocks, 0.0), axis=1)


def halves(value):
    high = value.astype(jnp.bfloat16)
    return high, (value - high.astype(jnp.float32)).astype(jnp.bfloat16)


def beside(high, low):
    return jnp.concatenate((high, low, high), axis=1)


def stack_parts(ref, row, value):
    rows = value.shape[0]
    high, low = halves(value)
    stride = ref.shape[0] // 3
    for part, kept in enumerate((high, high, low)):
        ref[pl.ds(row + part * stride, rows), :] = kept


def dot(left, right):
    return jnp.dot(left, right, preferred_element_type=jnp.float32)


def rotation_kernel(
    flags_ref, first_ref, second_ref, columns_ref, high_ref, low_ref,
    gen, square_ref, gen_parts, in_parts,
):
    width = first_ref.shape[0]
    size = 2 * width
    step = min(width, 256)
    first, second = first_ref[...], second_ref[...]
    first_t, second_t = first.T, second.T
    row, col = triangle_masks(width)
    gen[:width, :width] = jnp.where(row < col, first, jnp.where(row > col, -first_t, 0.0))
    gen[width:, width:] = jnp.where(row < col, second, jnp.where(row > col, -second_t, 0.0))
    gen[width:, :width] = jnp.where(row >= col, first, -second_t)
    gen[:width, width:] = jnp.where(row <= col, -first_t, second)
    for start in range(0, size, step):
        stack_parts(gen_parts, start, gen[start : start + step, :])

    def on_eye(index):
        row = lax.broadcasted_iota(jnp.int32, (step, size), 0) + index * step
        return row == lax.broadcasted_iota(jnp.int32, (step, size), 1)

    def square(index, carry):
        rows = pl.ds(pl.multiple_of(index * step, step), step)
        start = index * step
        high = gen_parts[pl.ds(pl.multiple_of(start, step), step), :]
        low = gen_parts[pl.ds(pl.multiple_of(start + 2 * size, step), step), :]
        product = dot(beside(high, low), gen_parts[...])
        square_ref[rows, :] = product
        value = gen[rows, :] * (1 / 6) + product * (1 / 24)
        value = value + jnp.where(on_eye(index), 0.5, 0.0)
        stack_parts(in_parts, pl.multiple_of(start, step), value)
        return carry

    lax.fori_loop(0, size // step, square, 0)
    swap_rows, swap_cols, chosen = flags_ref[0], flags_ref[1], flags_ref[2]

    def outer(index, carry):
        rows = pl.ds(pl.multiple_of(index * step, step), step)
        product = dot(beside(*halves(square_ref[rows, :])), in_parts[...])
        value = product + gen[rows, :] + jnp.where(on_eye(index), 1.0, 0.0)
        columns_ref[rows, :] = jnp.where(chosen == 0, value[:, :width], value[:, width:])
        turned = value.T
        per_half = width // step
        place = (index // per_half + swap_cols) % 2 * per_half + index % per_half
        cols = pl.ds(pl.multiple_of(place * step, step), step)
        for part in range(2):
            start = pl.multiple_of((part + swap_rows) % 2 * width, width)
            high, low = halves(turned[part * width : (part + 1) * width])
            high_ref[pl.ds(start, width), cols] = high
            low_ref[pl.ds(start, width), cols] = low
        return carry

    lax.fori_loop(0, size // step, outer, 0)


NO_COST = pl.CostEstimate(flops=0, bytes_accessed=0, transcendentals=0)


def rotation_of(first, second, swap_rows, swap_cols, chosen):
    width = first.shape[0]
    size = 2 * width
    whole = pl.BlockSpec(memory_space=pltpu.VMEM)
    flags = jnp.stack([jnp.asarray(flag, jnp.int32) for flag in (swap_rows, swap_cols, chosen)])
    return pl.pallas_call(
        rotation_kernel,
        out_shape=(
            jax.ShapeDtypeStruct((size, width), jnp.float32),
            jax.ShapeDtypeStruct((size, size), jnp.bfloat16),
            jax.ShapeDtypeStruct((size, size), jnp.bfloat16),
        ),
        in_specs=[pl.BlockSpec(memory_space=pltpu.SMEM), whole, whole],
        out_specs=(whole, whole, whole),
        scratch_shapes=[pltpu.VMEM((size, size), jnp.float32)] * 2
        + [pltpu.VMEM((3 * size, size), jnp.bfloat16)] * 2,
        compiler_params=pltpu.CompilerParams(vmem_limit_bytes=48 * 2**20),
        cost_estimate=NO_COST,
    )(flags, first, second)


def rotate_kernel(spans, per_half, *refs):
    step = pl.program_id(0)
    at = sum(count for side in spans for _, _, count in side)
    weights, turn_high, turn_low = refs[at : at + 2], refs[at + 2], refs[at + 3]
    outs = refs[at + 4 : -3]
    weight_parts, mid_parts = refs[-3:-1], refs[-1]
    block = turn_high.shape[0]
    first_part = 2 * per_half

    @pl.when(step == 0)
    def _():
        for side in range(2):
            stack_parts(weight_parts[side], 0, weights[side][...])

    for now in range(first_part):

        @pl.when(step == now)
        def _(now=now):
            total, at = None, 0
            for side in range(2):
                for first, steps, count in spans[side]:
                    if first <= now < first + steps:
                        value = refs[at][...]
                        for ref in refs[at + 1 : at + count]:
                            value = value + ref[...]
                        part = dot(beside(*halves(value)), weight_parts[side][...])
                        total = part if total is None else total + part
                    at += count
            stack_parts(mid_parts, now * block, total)

    @pl.when(step >= first_part)
    def _():
        product = dot(beside(turn_high[...], turn_low[...]), mid_parts[...])
        for half, out in enumerate(outs):

            @pl.when((step - first_part) // per_half == half)
            def _(out=out):
                out[...] = product


def block_rows(width):
    return min(width, 256)


def rotate(near, far, near_weights, far_weights, turn):
    width = near_weights.shape[0]
    size = 2 * width
    block = block_rows(width)
    per_half = width // block
    first_part = 2 * per_half
    turn_high, turn_low = turn
    out_halves = turn_high.shape[0] // width
    arrays, specs, spans = [], [], []
    for side in (near, far):
        span, first = [], 0
        for piece in side:
            steps = piece[0].shape[0] // block
            span.append((first, steps, len(piece)))

            def place(step, first=first, steps=steps):
                return jnp.clip(step - first, 0, steps - 1), 0

            for array in piece:
                arrays.append(array)
                specs.append(pl.BlockSpec((block, width), place))
            first += steps
        spans.append(tuple(span))
    fixed = pl.BlockSpec((width, width), lambda step: (0, 0))
    turning = pl.BlockSpec(
        (block, size),
        lambda step: (jnp.clip(step - first_part, 0, out_halves * per_half - 1), 0),
    )
    outs = [
        pl.BlockSpec(
            (block, width),
            lambda step, half=half: (
                jnp.clip(step - first_part - half * per_half, 0, per_half - 1),
                0,
            ),
        )
        for half in range(out_halves)
    ]
    return pl.pallas_call(
        functools.partial(rotate_kernel, tuple(spans), per_half),
        grid=(first_part + out_halves * per_half,),
        out_shape=[jax.ShapeDtypeStruct((width, width), jnp.float32)] * out_halves,
        in_specs=[*specs, fixed, fixed, turning, turning],
        out_specs=outs,
        scratch_shapes=[pltpu.VMEM((3 * width, width), jnp.bfloat16)] * 2
        + [pltpu.VMEM((3 * size, width), jnp.bfloat16)],
        compiler_params=pltpu.CompilerParams(vmem_limit_bytes=40 * 2**20),
        cost_estimate=NO_COST,
    )(*arrays, near_weights, far_weights, turn_high, turn_low)


def rows_of(value, which, width):
    return lax.dynamic_slice_in_dim(value, which * width, width, value.ndim - 2)


def first_generator(grid, tiles, own_centres, other_centres):
    width = tiles.shape[2]
    is_first = grid.parity == 0
    centres = jnp.where(
        is_first,
        jnp.concatenate((own_centres, other_centres), axis=1),
        jnp.concatenate((other_centres, own_centres), axis=1),
    )
    generator = STEP_SIZE * jnp.sum(
        tiles * (own_centres[:, None, :] - centres[:, :, None]), axis=0
    )
    row, col = triangle_masks(width)
    top, bottom = generator[:width], generator[width:]
    return jnp.where(
        is_first, jnp.where(row < col, top, bottom), jnp.where(row < col, bottom, top)
    )


def second_generator(grid, blocks, own_centres, row_centres, col_centres):
    same = grid.row_high == grid.col_high
    row_centres = jnp.where(same, own_centres, row_centres)
    col_centres = jnp.where(same, own_centres, col_centres)
    return STEP_SIZE * jnp.sum(
        blocks * (col_centres[:, None, :] - row_centres[:, :, None]), axis=0
    )


def local(positions):
    grid = Grid(lax.axis_size("row"), lax.axis_size("col"))
    count, height, width = positions.shape
    half = count // 2
    block = block_rows(width)
    early, late = list(range(half)), list(range(half, count))
    is_first = grid.parity == 0
    is_low = grid.row_high == 0
    is_left = grid.col_high == 0
    same = grid.row_high == grid.col_high
    groups = grid.groups > 1

    def weights_of(columns, which):
        return rows_of(columns, which, width), rows_of(columns, 1 - which, width)

    raw_queue = [(k, row) for k in early for row in range(0, height, block)]
    raw = {k: [] for k in early}

    def send_raw(pieces, token):
        arrived = []
        for k, row in raw_queue[:pieces]:
            rows = after(positions[k, row : row + block], token)
            arrived.append(grid.swap_col_high(rows))
            raw[k].append(arrived[-1])
        del raw_queue[:pieces]
        return arrived

    urgent, rest = [None] * count, {}

    def send_urgent(k, *tokens):
        urgent[k] = grid.swap_parity(after(positions[k], *tokens), on_group)

    def send_rest(k, *tokens):
        rest[k] = grid.swap_parity(after(positions[k], *tokens), off_group) if groups else None

    def rests(k):
        return [rest[k]] if groups else []

    own_centres = diagonal(rows_of(positions, grid.parity, width))
    other_centres = grid.swap_parity(own_centres, on_pair)
    packed = first_generator(grid, positions, own_centres, other_centres)
    send_rest(late[0], other_centres)
    packed = jnp.where(same, packed, grid.swap_col_high(packed, on_pair))
    packed = after(packed, *rests(late[0]))
    send_rest(late[1], packed)
    packed = grid.spread_col_group(packed)
    packed = after(packed, *rests(late[1]))
    pieces = send_raw(1, packed)
    other = after(grid.swap_parity(packed), *pieces)
    send_urgent(0, other)
    pieces = send_raw(1, other)
    columns, *turn = rotation_of(
        jnp.where(is_first, packed, other),
        jnp.where(is_first, other, packed),
        grid.row_high,
        0,
        grid.parity,
    )
    columns = after(columns, urgent[0], *pieces)
    send_urgent(1, columns)
    send_rest(early[0], columns)
    pieces = send_raw(2, columns)
    arrived = grid.swap_row_high(columns, on_group)
    columns = jnp.stack((jnp.where(same, columns, arrived), jnp.where(same, arrived, columns)))
    columns = after(columns, *pieces, urgent[1], *rests(early[0]))
    send_urgent(2, columns)
    send_urgent(3, columns)
    pieces = send_raw(2, columns)
    columns = grid.spread_row_group(columns)
    near_weights = weights_of(columns[0], grid.parity)
    far_weights = weights_of(columns[1], grid.parity)

    block_turn = [rows_of(part, grid.parity ^ grid.row_high, width) for part in turn]
    blocks = jnp.stack(
        [
            rotate([[positions[k]]], [[urgent[k]]], *near_weights, block_turn)[0]
            for k in range(count)
        ]
    )
    blocks = after(blocks, *pieces)
    pieces = send_raw(len(raw_queue), blocks)
    send_rest(early[1], blocks)
    own_centres = diagonal(blocks)
    row_centres = grid.swap_col_high(own_centres, on_pair)
    col_centres = grid.swap_row_high(own_centres, on_pair)
    own = second_generator(grid, blocks, own_centres, row_centres, col_centres)
    other = grid.swap_row_high(own, lambda rh, rg, ch, cg, e: rg == cg and rh != e)

    near, sent, moved = {}, {}, {}

    def first_round(k, token):
        partner = [urgent[k], *rests(k)]
        tile = after(positions[k], token)
        near[k], sent[k] = rotate([[tile]], [partner], *near_weights, turn)

    def move(k, token):
        moved[k] = grid.swap_row_high(after(sent[k], token))

    away = grid.send(own, grid.rows // 2, 1, lambda rh, rg, ch, cg, e: rg == cg and rh != e)
    beside_own = grid.swap_parity(own, lambda rh, rg, ch, cg, e: rg == cg and rh == e)
    at_home = grid.parity == grid.row_high
    mine, theirs = jnp.where(at_home, own, beside_own), jnp.where(at_home, other, away)
    first_round(late[0], blocks)
    move(late[0], own)
    first_round(late[1], own)
    top, bottom = jnp.where(is_low, mine, theirs), jnp.where(is_low, theirs, mine)
    row, col = triangle_masks(width)
    packed = jnp.where(
        is_left, jnp.where(row < col, top, bottom), jnp.where(row < col, bottom, top)
    )
    packed = after(packed, near[late[1]], moved[late[0]], *pieces)
    packed = after(packed, *rests(early[1]))
    other = grid.swap_col_high(packed, on_group)
    move(late[1], packed)
    first_round(early[0], packed)
    move(early[0], packed)
    first_round(early[1], packed)
    far_queue = [(k, part) for k in early for part in range(2)]
    far_partner = {k: [] for k in early}

    def send_far(token):
        k, part = far_queue.pop(0)
        pieces = raw[k][part * len(raw[k]) // 2 : (part + 1) * len(raw[k]) // 2]
        rows = jnp.concatenate(pieces, axis=0)
        far_partner[k].append(grid.swap_parity(after(rows, token)))
        return far_partner[k][-1]

    late_far = {k: [] for k in late}

    def send_late(k, part, token):
        late_far[k].append(grid.swap_col_high(after(part, token)))
        return late_far[k][-1]

    middle = width // 2
    pieces = [send_late(late[0], near[late[0]][:middle], packed)]
    partner = [send_far(packed), send_far(packed)]
    both = jnp.stack((jnp.where(is_left, packed, other), jnp.where(is_left, other, packed)))
    both = after(both, moved[late[1]], moved[early[0]], near[early[1]], *pieces, *partner)
    parts = (near[late[0]][middle:], moved[late[0]][:middle])
    late_half = send_late(late[0], jnp.concatenate(parts, axis=0), both)
    partner = send_far(both)
    move(early[1], both)
    far_near, far_sent, far_moved = {}, {}, {}

    def far_round(k, token):
        tiles = [[after(part, token)] for part in raw[k]]
        others = [[part] for part in far_partner[k]]
        far_near[k], far_sent[k] = rotate(tiles, others, *far_weights, turn)

    def far_move(k, token):
        far_moved[k] = grid.swap_row_high(after(far_sent[k], token))

    far_round(early[0], both)
    both = grid.spread_col_group(both)
    both = after(both, far_near[early[0]], moved[early[1]], partner)
    late_quarter = send_late(late[0], moved[late[0]][middle:], both)
    far_move(early[0], both)
    partner = send_far(both)
    columns, *second_turn = rotation_of(
        both[0], both[1], grid.row_high, grid.row_high, grid.col_high
    )
    columns = after(columns, far_moved[early[0]], late_half, partner)
    far_round(early[1], columns)
    arrived = grid.swap_row_high(columns, lambda rh, rg, ch, cg, e: rg == cg and rh == e)
    columns = jnp.where(grid.row_high == grid.parity, columns, arrived)
    columns = after(columns, far_near[early[1]], late_quarter)
    far_move(early[1], columns)
    first_quarter = send_late(late[1], near[late[1]][:middle], columns)
    weights = weights_of(grid.spread_row_group(columns), grid.col_high)
    weights = [after(weight, first_quarter) for weight in weights]
    parts = (near[late[1]][middle:], moved[late[1]])
    send_late(late[1], jnp.concatenate(parts, axis=0), first_quarter)

    outputs = [None] * count
    before = [far_moved[early[1]]]
    for k in [*early, *late]:
        mine = [[near[k]], [moved[k]]]
        theirs = [[far_near[k]], [far_moved[k]]] if k in early else [[part] for part in late_far[k]]
        kept, leaving = rotate(mine, theirs, *weights, second_turn)
        arrived = grid.swap_row_high(leaving)
        if k == late[0]:
            before.append(arrived)
        weights = [after(weight, kept, *before) for weight in weights]
        before = [arrived]
        outputs[k] = [jnp.where(is_low, kept, arrived), jnp.where(is_low, arrived, kept)]
    return jnp.stack([part for pair in outputs for part in pair]).reshape(positions.shape)


def solution(mesh):
    spec = P(None, "row", "col")
    return jax.shard_map(local, mesh=mesh, in_specs=(spec,), out_specs=spec, check_vma=False)
```
